32 devices in a mesh: req: 8 (over y, x, core), head: 4 (over z).
Axes of the slice: x: 2, y: 2, z: 4, core: 2. Of those that a mesh axis runs over, the one named last changes fastest.
Arguments:
- hidden_in: bfloat16 [2048, 2048], P(('req', 'head')), may hold values from -6 to 6
- segment_ids: int32 [8, 256], P('req', 'head'), may hold values from 0 to 3, never falling along the last dimension, each value on 1 to 128 neighbouring positions
- attn_routes: int32 [2048, 2], P(('req', 'head')), may hold values from 0 to 7, all different within a row; in each aligned block of 256 rows (0 to 255, 256 to 511, ...) at most 96 rows name the same one
- ffn_routes: int32 [2048, 2], P(('req', 'head')), may hold values from 0 to 7, all different within a row; in each aligned block of 64 rows (0 to 63, 64 to 127, ...) at most 24 rows name the same one
- attn_gain: float32 [2048], replicated, may hold values from 0.1 to 1.9
- attn_router: float32 [2048, 8], replicated, may hold values from -0.125 to 0.125
- w_query: bfloat16 [8, 2048, 2048], P(None, None, 'head'), may hold values from -1 to 1
- w_key: bfloat16 [2048, 2048], P(None, 'head'), may hold values from -32 to 32
- w_value: bfloat16 [2048, 2048], P(None, 'head'), may hold values from -0.125 to 0.125
- w_out: bfloat16 [8, 2048, 2048], P(None, 'head'), may hold values from -0.125 to 0.125
- ffn_gain: float32 [2048], replicated, may hold values from 0.1 to 1.9
- ffn_router: float32 [2048, 8], replicated, may hold values from -0.125 to 0.125
- w_gate_up: bfloat16 [8, 2048, 2, 5632], P('head', None, None, 'req'), may hold values from -0.125 to 0.125
- w_down: bfloat16 [8, 5632, 2048], P('head', 'req'), may hold values from -0.078125 to 0.078125
Outputs:
- layer_out: bfloat16 [2048, 2048], P(('req', 'head'))
The draws below stay inside these ranges and needn't reach their ends.
Inputs may be any that keep to these rules, and one draw needn't show every extreme that they name: `segment_ids`: within each row segment numbers never fall; each segment has 1 to 128 tokens. `attn_routes`: each token names two different experts; in each aligned block of 256 rows no expert is named by more than 96 rows. `ffn_routes`: each token names two different experts; in each aligned block of 64 rows (the rows of one device) no expert is named by more than 24 rows.
All inputs are finite; a program needn't handle non-finite values.
Results may differ from the reference program's by a relative error of at most 0.015.
Values may be sent and summed in bfloat16 or wider, within the bound.
A program may use at most 128 MiB of HBM per device.

```python
import math
import jax
import jax.numpy as jnp
import numpy as np
from jax import lax

D = 2048
FF = 5632
H_KV = 16
HD = 128
E_ATT = 8
E_FF = 8
TOK_DEV = 64
TOK_REQ = 256
TOKENS = 2048
CAP_ATT = 96
C_FF = 24
N_REQ = 8
N_HEAD = 4


def paired_weights(random_key):
    base_key = jax.random.fold_in(random_key, 7)
    query_key, noise_key = jax.random.split(base_key, 2)
    queries = jnp.clip(jax.random.normal(query_key, (E_ATT, D, H_KV * HD), jnp.float32), -6.0, 6.0) * D ** (-0.5)
    noise = jnp.clip(jax.random.normal(noise_key, (D, H_KV * HD), jnp.float32), -6.0, 6.0) * D ** (-0.5)
    return (queries, noise)


def draw_w_query(key, part):
    queries, noise = paired_weights(key)
    return queries.astype(jnp.bfloat16)


def draw_w_key(key, part):
    queries, noise = paired_weights(key)
    return noise.astype(jnp.bfloat16)


def block_levels(stream_key, dims, cuts, smallest, high):
    level = 1.0
    for position, shards_of in cuts:
        heights = jax.random.uniform(jax.random.fold_in(jax.random.fold_in(stream_key, 6), position), (shards_of,), jnp.float32, smallest / len(cuts), high / len(cuts))
        level = level * jnp.repeat(jnp.exp(heights), dims[position] // shards_of).reshape((-1,) + (1,) * (len(dims) - 1 - position))
    return level


def split_up(count, total, reach, slope):
    weights = [(1 << 20) // math.isqrt(standing ** slope) + 1 for standing in range(2, count + 1)]
    surplus, holding = total - reach - (count - 1), [1] * (count - 1)
    while surplus > 0:
        free = [i for i in range(count - 1) if holding[i] < reach]
        mass, budget = sum([weights[i] for i in free]), surplus
        for i in free:
            addition = min(reach - holding[i], max(1, budget * weights[i] // mass), surplus)
            holding[i] = holding[i] + addition
            surplus = surplus - addition
    return np.array([reach] + holding)


def ragged_sizes(rng, amount, total, most, lean):
    if amount == 2:
        one = jax.random.randint(rng, (), max(1, total - most), min(most, total - 1) + 1)
        return jnp.stack([one, total - one])
    tallies = jnp.asarray(split_up(amount, total, most, lean), jnp.int32)
    pairs = (amount - 1) // 2
    source_of, receiver = tallies[1:1 + 2 * pairs:2], tallies[2:2 + 2 * pairs:2]
    room = jnp.minimum(source_of - 1, most - receiver)
    passed = jax.random.randint(jax.random.fold_in(rng, 1), (pairs,), 0, 1 << 20) % (room + 1)
    tallies = tallies.at[1:1 + 2 * pairs:2].set(source_of - passed).at[2:2 + 2 * pairs:2].set(receiver + passed)
    return tallies[jax.random.permutation(jax.random.fold_in(rng, 2), amount)]


def routed_block(key, own, number, rows, number_of, top, reach, slope):
    ranking = jax.random.permutation(key, number_of)
    heavy_load, usual = shares(number_of, rows * top, reach, slope, True), shares(number_of, rows * top, reach, slope, False)
    places = jnp.arange(number_of)

    def named(sizes, offset_by):
        used = int((sizes > 0).sum())
        fixed = max(1, used // 4)
        shifted = fixed + (places - fixed + offset_by * (used - fixed)) % max(1, number_of - fixed)
        return jnp.zeros((number_of,), jnp.int32).at[ranking[jnp.where(places < fixed, places, shifted)]].set(jnp.asarray(sizes, jnp.int32))

    sizes = jnp.where(number % 4 == 0, named(heavy_load, number // 4), named(usual, number - number // 4 - 1))
    mixed = jax.random.permutation(jax.random.fold_in(own, 3), number_of)
    source_of, receiver = mixed[0:number_of // 2 * 2:2], mixed[1:number_of // 2 * 2:2]
    slack = jnp.minimum(sizes[source_of] - 1, reach - sizes[receiver]) // 2
    slack = jnp.where((source_of == ranking[0]) | (receiver == ranking[0]) | (sizes[receiver] == 0), 0, jnp.maximum(slack, 0))
    shifted = jax.random.randint(jax.random.fold_in(own, 4), (number_of // 2,), 0, 1 << 20) % (slack + 1)
    sizes = sizes.at[source_of].add(-shifted).at[receiver].add(shifted)
    labels = jnp.searchsorted(jnp.cumsum(sizes), jnp.arange(rows * top), side="right").astype(jnp.int32)
    grid = labels.reshape(top, rows).T
    grid = grid[jax.random.permutation(jax.random.fold_in(own, 1), rows)]
    offset_by = jax.random.randint(jax.random.fold_in(own, 2), (rows, 1), 0, top)
    return jnp.take_along_axis(grid, (jnp.arange(top)[None, :] + offset_by) % top, axis=1)


def shares(count, total, reach, skew, full):
    weights = [(1 << 20) // math.isqrt(grade ** skew) + 1 for grade in range(1, count + 1)]
    largest = reach if full else min(reach, max(-(-total // count), total * weights[0] // sum(weights)))
    least = 1 if total - largest >= count - 1 else 0
    counts, rest = [largest] + [least] * (count - 1), total - largest - least * (count - 1)
    while rest > 0:
        movable = [i for i in range(1, count) if counts[i] < largest] or [i for i in range(1, count) if counts[i] < reach]
        pool, remaining = sum([weights[i] for i in movable]), rest
        for i in movable:
            more = min(reach - counts[i], max(1, remaining * weights[i] // pool), rest)
            counts[i] = counts[i] + more
            rest = rest - more
    return np.array(counts)


def gaussian(key, extent, spread, limit, cuts=(), held_as=jnp.bfloat16):
    drawn = jax.random.normal(key, extent, jnp.float32) * spread
    if len(cuts) > 0:
        drawn = block_levels(key, extent, cuts, -0.22, 0.18) * drawn
    return jnp.clip(drawn, min=-limit, max=limit).astype(held_as)


def setup_inputs(seed: int = 0) -> dict:
    splits = jax.random.split(jax.random.key(seed), 15)
    hidden_in = gaussian(splits[0], (TOKENS, D), 1.0, 6.0, ((0, 32),))
    segment_ids = jax.vmap(lambda own: jnp.searchsorted(jnp.cumsum(ragged_sizes(own, 4, TOK_REQ, TOK_REQ // 2, 2)), jnp.arange(TOK_REQ), side="right"))(jax.random.split(splits[1], N_REQ)).reshape((N_REQ, TOK_REQ)).astype(jnp.int32)
    attn_routes_keys = jax.random.split(jax.random.fold_in(splits[2], 1), TOKENS // TOK_REQ)
    attn_routes_turns = jax.random.permutation(jax.random.fold_in(splits[2], 3), TOKENS // TOK_REQ)
    attn_routes = jax.vmap(lambda own, number: routed_block(jax.random.fold_in(splits[2], 2), own, number, TOK_REQ, E_ATT, 2, CAP_ATT, 1))(attn_routes_keys, attn_routes_turns).reshape((TOKENS, 2))
    ffn_routes_keys = jax.random.split(jax.random.fold_in(splits[3], 1), TOKENS // TOK_DEV)
    ffn_routes_turns = jax.random.permutation(jax.random.fold_in(splits[3], 3), TOKENS // TOK_DEV)
    ffn_routes = jax.vmap(lambda own, number: routed_block(jax.random.fold_in(splits[3], 2), own, number, TOK_DEV, E_FF, 2, C_FF, 1))(ffn_routes_keys, ffn_routes_turns).reshape((TOKENS, 2))
    attn_gain = jnp.clip(1.0 + 0.18 * jax.random.normal(splits[4], (D,), jnp.float32), 0.1, 1.9)
    attn_router = gaussian(splits[5], (D, E_ATT), D ** -0.5, 0.125, (), jnp.float32)
    w_query = draw_w_query(jax.random.fold_in(splits[14], 71), 0)
    w_key = draw_w_key(jax.random.fold_in(splits[14], 71), 0)
    w_value = gaussian(splits[8], (D, H_KV * HD), D ** -0.5, 0.125, ((1, 4),))
    w_out = gaussian(splits[9], (E_ATT, H_KV * HD, D), (H_KV * HD) ** -0.5, 0.125, ((1, 4),))
    ffn_gain = jnp.clip(1.0 + 0.18 * jax.random.normal(splits[10], (D,), jnp.float32), 0.1, 1.9)
    ffn_router = gaussian(splits[11], (D, E_FF), D ** -0.5, 0.125, (), jnp.float32)
    w_gate_up = gaussian(splits[12], (E_FF, D, 2, FF), D ** -0.5, 0.125, ((0, 4), (3, 8)))
    w_down = gaussian(splits[13], (E_FF, FF, D), FF ** -0.5, 0.078125, ((0, 4), (1, 8)))
    return dict(hidden_in=hidden_in, segment_ids=segment_ids, attn_routes=attn_routes, ffn_routes=ffn_routes, attn_gain=attn_gain, attn_router=attn_router, w_query=w_query, w_key=w_key, w_value=w_value, w_out=w_out, ffn_gain=ffn_gain, ffn_router=ffn_router, w_gate_up=w_gate_up, w_down=w_down)


EPSILON = 1e-06
ROPE_BASE = 10000.0

def rms_norm(values, gain_vector):
    widened = values.astype(jnp.float32)
    inverse_rms = lax.rsqrt(lax.optimization_barrier(jnp.mean(widened * widened, axis=-1, keepdims=True)) + EPSILON)
    return (widened * inverse_rms * gain_vector).astype(jnp.bfloat16)

def pair_gates(normed, router, routes):
    logits = jnp.dot(normed.astype(jnp.float32), router, precision=lax.Precision.HIGHEST)
    picked = jnp.take_along_axis(logits, routes, axis=1)
    first_weight = jax.nn.sigmoid(picked[:, 0] - picked[:, 1])
    second_weight = jax.nn.sigmoid(picked[:, 1] - picked[:, 0])
    return jnp.stack([first_weight, second_weight], axis=1)

def positions(segment_row):
    earlier = (segment_row[None, :] < segment_row[:, None]).astype(jnp.int32)
    return (jnp.arange(segment_row.shape[0], dtype=jnp.int32) - lax.optimization_barrier(jnp.sum(earlier, axis=1))).astype(jnp.int32)

def rotary(values, token_place):
    half_width = values.shape[-1] // 2
    inverse = ROPE_BASE ** (-jnp.arange(half_width, dtype=jnp.float32) / half_width)
    shaped = token_place.astype(jnp.float32).reshape((-1,) + (1,) * (values.ndim - 2) + (1,))
    angles = shaped * inverse
    cosine = jnp.cos(angles)
    sines = jnp.sin(angles)
    lower_half = values[..., :half_width]
    upper_half = values[..., half_width:]
    return jnp.concatenate([lower_half * cosine - upper_half * sines, upper_half * cosine + lower_half * sines], axis=-1)

def slot_ranks(experts_flat, expert_count):
    onehot = (experts_flat[:, None] == jnp.arange(expert_count, dtype=jnp.int32)[None, :]).astype(jnp.int32)
    running = jnp.cumsum(onehot, axis=0) - onehot
    return lax.optimization_barrier(jnp.sum(running * onehot, axis=1)).astype(jnp.int32)

def soft_weights(scores, allowed):
    masked = jnp.where(allowed, scores, -1e+30)
    largest = lax.optimization_barrier(jnp.max(masked, axis=-1, keepdims=True))
    exponent = jnp.exp(masked - largest)
    return (exponent / lax.optimization_barrier(jnp.sum(exponent, axis=-1, keepdims=True))).astype(jnp.bfloat16)

def reference(hidden_in, segment_ids, attn_routes, ffn_routes, attn_gain, attn_router, w_query, w_key, w_value, w_out, ffn_gain, ffn_router, w_gate_up, w_down):
    seq_length = TOK_REQ
    capacity = CAP_ATT
    width = H_KV * HD
    normed = rms_norm(hidden_in, attn_gain)
    query_weights = w_query.astype(jnp.float32)
    out_weights = w_out.astype(jnp.float32)

    def attend_block(block_input):
        block_normed, segment_row, block_routes = block_input
        pair_weights = pair_gates(block_normed, attn_router, block_routes)
        token_place = positions(segment_row)
        flat_experts = block_routes.reshape(-1)
        slot_index = flat_experts * capacity + slot_ranks(flat_experts, E_ATT)
        slot_table = jnp.full((E_ATT * capacity,), 2 * seq_length, jnp.int32).at[slot_index].set(jnp.arange(2 * seq_length, dtype=jnp.int32))
        padded = jnp.concatenate([block_normed, jnp.zeros((1, D), jnp.bfloat16)], axis=0)
        buffer = padded[slot_table // 2].reshape(E_ATT, capacity, D)
        query_buf = jnp.einsum('ecd,edf->ecf', buffer.astype(jnp.float32), query_weights)
        queries = query_buf.reshape(E_ATT * capacity, width)[slot_index].reshape(seq_length, 2, H_KV, HD)
        queries = rotary(queries, token_place).astype(jnp.bfloat16)
        key_heads = jnp.dot(block_normed, w_key, preferred_element_type=jnp.float32).reshape(seq_length, H_KV, HD)
        key_heads = rotary(key_heads, token_place).astype(jnp.bfloat16)
        value_heads = jnp.dot(block_normed, w_value, preferred_element_type=jnp.float32).astype(jnp.bfloat16).reshape(seq_length, H_KV, HD)
        scores = jnp.einsum('tjhd,shd->hjts', queries.astype(jnp.float32), key_heads.astype(jnp.float32)) * HD ** (-0.5)
        indices = jnp.arange(seq_length, dtype=jnp.int32)
        allowed = (segment_row[:, None] == segment_row[None, :]) & (indices[None, :] <= indices[:, None])
        probs = soft_weights(scores, allowed)
        context = jnp.einsum('hjts,shd->tjhd', probs.astype(jnp.float32), value_heads.astype(jnp.float32)).astype(jnp.bfloat16)
        padded_ctx = jnp.concatenate([context.reshape(2 * seq_length, width), jnp.zeros((1, width), jnp.bfloat16)], axis=0)
        out_buf = padded_ctx[slot_table].reshape(E_ATT, capacity, width)
        projected = jnp.einsum('ecf,efd->ecd', out_buf.astype(jnp.float32), out_weights)
        per_pair = projected.reshape(E_ATT * capacity, D)[slot_index] * pair_weights.reshape(-1)[:, None]
        return lax.optimization_barrier(jnp.sum(per_pair.reshape(seq_length, 2, D), axis=1))
    attended = lax.map(attend_block, (normed.reshape(N_REQ, seq_length, D), segment_ids, attn_routes.reshape(N_REQ, seq_length, 2)))
    residual = (hidden_in.astype(jnp.float32) + attended.reshape(TOKENS, D)).astype(jnp.bfloat16)
    ffn_normed = rms_norm(residual, ffn_gain)
    ffn_weights = pair_gates(ffn_normed, ffn_router, ffn_routes)
    total_cap = N_REQ * N_HEAD * C_FF
    flat_experts = ffn_routes.reshape(-1)
    slot_index = flat_experts * total_cap + slot_ranks(flat_experts, E_FF)
    slot_table = jnp.full((E_FF * total_cap,), 2 * TOKENS, jnp.int32).at[slot_index].set(jnp.arange(2 * TOKENS, dtype=jnp.int32))
    padded = jnp.concatenate([ffn_normed, jnp.zeros((1, D), jnp.bfloat16)], axis=0)
    shard_width = FF // N_REQ

    def expert_block(expert_input):
        expert_table, gate_up, down_weights = expert_input
        rows_in = padded[expert_table // 2]
        gate_and_up = jnp.dot(rows_in, gate_up.reshape(D, 2 * FF), preferred_element_type=jnp.float32).reshape(total_cap, 2, FF)
        activation = (jax.nn.silu(gate_and_up[:, 0]) * gate_and_up[:, 1]).astype(jnp.bfloat16)
        shard_acts = activation.reshape(total_cap, N_REQ, shard_width).transpose(1, 0, 2)
        shard_downs = down_weights.reshape(N_REQ, shard_width, D)

        def add_shard(running_total, shard_input):
            act_shard, down_shard = shard_input
            partials = jnp.dot(act_shard, down_shard, preferred_element_type=jnp.float32).astype(jnp.bfloat16)
            return (running_total + lax.optimization_barrier(partials).astype(jnp.float32), jnp.zeros((), jnp.float32))
        summed, unused = lax.scan(add_shard, jnp.zeros((total_cap, D), jnp.float32), (shard_acts, shard_downs))
        return summed.astype(jnp.bfloat16)
    expert_out = lax.map(expert_block, (slot_table.reshape(E_FF, total_cap), w_gate_up, w_down))
    gathered = expert_out.reshape(E_FF * total_cap, D)[slot_index]
    mixture = lax.optimization_barrier(jnp.sum(gathered.astype(jnp.float32).reshape(TOKENS, 2, D) * ffn_weights[:, :, None], axis=1))
    return (residual.astype(jnp.float32) + mixture).astype(jnp.bfloat16)
```

```python
import functools

import jax
import jax.numpy as jnp
from jax import lax
from jax.experimental import pallas as pl
from jax.experimental.pallas import tpu as pltpu
from jax.sharding import PartitionSpec as P

D = 2048
HD = 128
E_ATT = 8
E_FF = 8


EPSILON = 1e-06
ROPE_BASE = 10000.0


def rms_norm(values, gain_vector):
    widened = values.astype(jnp.float32)
    inverse_rms = lax.rsqrt(jnp.mean(widened * widened, axis=-1, keepdims=True) + EPSILON)
    return (widened * inverse_rms * gain_vector).astype(jnp.bfloat16)


def pair_gates(normed, router, routes):
    logits = jnp.dot(normed.astype(jnp.float32), router, precision=lax.Precision.HIGHEST)
    experts = jnp.arange(router.shape[1], dtype=jnp.int32)
    onehot = (routes[:, :, None] == experts).astype(jnp.float32)
    picked = jnp.sum(onehot * logits[:, None, :], axis=2)
    return jax.nn.sigmoid(picked - picked[:, ::-1])


def positions(segment_row):
    earlier = (segment_row[None, :] < segment_row[:, None]).astype(jnp.int32)
    return jnp.arange(segment_row.shape[0], dtype=jnp.int32) - jnp.sum(earlier, axis=1)


def rotary_table(token_place):
    half_width = HD // 2
    inverse = ROPE_BASE ** (-jnp.arange(half_width, dtype=jnp.float32) / half_width)
    angles = token_place.astype(jnp.float32)[:, None] * inverse
    cosine = jnp.cos(angles)
    sines = jnp.sin(angles)
    return jnp.concatenate([cosine, cosine, -sines, sines], axis=1)


def rotate(head, table):
    return head * table[:, :HD] + pltpu.roll(head, HD // 2, 1) * table[:, HD:]


def attention_kernel(
    capacity, rows_ref, info_ref, table_ref, w_key_ref, w_value_ref, w_query_ref, w_out_ref,
    out_ref, keys, values, total,
):
    expert = pl.program_id(0)
    seq = rows_ref.shape[0]
    heads = w_key_ref.shape[1] // HD
    rows = rows_ref[...]

    @pl.when(expert == 0)
    def _():
        raw_keys = jnp.dot(rows, w_key_ref[...], preferred_element_type=jnp.float32)
        for head in range(heads):
            part = raw_keys[:, head * HD : (head + 1) * HD]
            keys[:, head * HD : (head + 1) * HD] = rotate(part, table_ref[...]).astype(jnp.bfloat16)
        values[...] = jnp.dot(
            rows, w_value_ref[...], preferred_element_type=jnp.float32
        ).astype(jnp.bfloat16)
        total[...] = jnp.zeros_like(total)

    own = expert.astype(jnp.float32)
    first, second = info_ref[0:1, :] == own, info_ref[1:2, :] == own
    member = (first | second).astype(jnp.float32)
    gates = jnp.where(first, info_ref[2:3, :], jnp.where(second, info_ref[3:4, :], 0.0))
    segments = info_ref[4:5, :]
    earlier = (
        lax.broadcasted_iota(jnp.int32, (seq, seq), 0)
        < lax.broadcasted_iota(jnp.int32, (seq, seq), 1)
    ).astype(jnp.float32).astype(jnp.bfloat16)
    rank = jnp.dot(
        jnp.broadcast_to(member, (16, seq)).astype(jnp.bfloat16), earlier,
        preferred_element_type=jnp.float32,
    )[0:1, :]
    slots = lax.broadcasted_iota(jnp.int32, (capacity, seq), 0).astype(jnp.float32)
    place = lax.broadcasted_iota(jnp.int32, (capacity, seq), 1).astype(jnp.float32)
    pick = jnp.where((slots == rank) & (member > 0.0), 1.0, 0.0)
    pick_half = pick.astype(jnp.bfloat16)
    slot_gate = jnp.sum(pick * gates, axis=1, keepdims=True)
    slot_segment = jnp.sum(pick * segments, axis=1, keepdims=True)
    slot_place = jnp.sum(pick * place, axis=1, keepdims=True)
    slot_table = jnp.dot(
        pick, table_ref[...], precision=lax.Precision.HIGHEST, preferred_element_type=jnp.float32
    )
    allowed = (slot_segment == segments) & (place <= slot_place)
    picked = jnp.dot(pick_half, rows, preferred_element_type=jnp.float32).astype(jnp.bfloat16)
    raw = jnp.dot(picked, w_query_ref[0], preferred_element_type=jnp.float32)
    contexts = []
    for head in range(heads):
        span = slice(head * HD, (head + 1) * HD)
        query = rotate(raw[:, span], slot_table).astype(jnp.bfloat16)
        scores = lax.dot_general(
            query, keys[:, span], (((1,), (1,)), ((), ())), preferred_element_type=jnp.float32
        ) * HD ** (-0.5)
        masked = jnp.where(allowed, scores, -1e30)
        exponent = jnp.exp(masked - jnp.max(masked, axis=1, keepdims=True))
        probs = (exponent / jnp.sum(exponent, axis=1, keepdims=True)).astype(jnp.bfloat16)
        contexts.append(
            jnp.dot(probs, values[:, span], preferred_element_type=jnp.float32).astype(jnp.bfloat16)
        )
    context = jnp.concatenate(contexts, axis=1)
    projected = jnp.dot(context, w_out_ref[0], preferred_element_type=jnp.float32)
    weighted = (projected * slot_gate).astype(jnp.bfloat16)
    total[...] += lax.dot_general(
        pick_half, weighted, (((0,), (0,)), ((), ())), preferred_element_type=jnp.float32
    )

    @pl.when(expert == pl.num_programs(0) - 1)
    def _():
        out_ref[...] = total[...].astype(jnp.bfloat16)


def attention(rows, info, table, w_key, w_value, w_query, w_out, capacity):
    seq, width = rows.shape[0], w_key.shape[1]
    whole = lambda shape: pl.BlockSpec(shape, lambda e: (0,) * len(shape))
    return pl.pallas_call(
        functools.partial(attention_kernel, capacity),
        grid=(E_ATT,),
        out_shape=jax.ShapeDtypeStruct((seq, D), jnp.bfloat16),
        in_specs=[
            whole((seq, D)),
            whole(info.shape),
            whole(table.shape),
            whole((D, width)),
            whole((D, width)),
            pl.BlockSpec((1, D, width), lambda e: (e, 0, 0)),
            pl.BlockSpec((1, width, D), lambda e: (e, 0, 0)),
        ],
        out_specs=whole((seq, D)),
        scratch_shapes=[
            pltpu.VMEM((seq, width), jnp.bfloat16),
            pltpu.VMEM((seq, width), jnp.bfloat16),
            pltpu.VMEM((seq, D), jnp.float32),
        ],
        compiler_params=pltpu.CompilerParams(vmem_limit_bytes=48 * 1024 * 1024),
        cost_estimate=pl.CostEstimate(
            flops=12 * 10**9, bytes_accessed=40 * 10**6, transcendentals=10**6
        ),
    )(rows, info, table, w_key, w_value, w_query, w_out)


def per_device(
    hidden_in,
    segment_ids,
    attn_routes,
    ffn_routes,
    attn_gain,
    attn_router,
    w_query,
    w_key,
    w_value,
    w_out,
    ffn_gain,
    ffn_router,
    w_gate_up,
    w_down,
):
    row_count = hidden_in.shape[0]
    head_count = lax.axis_size("head")
    seq_length = row_count * head_count
    capacity = 3 * seq_length // 8
    normed = rms_norm(hidden_in, attn_gain)
    labels = jnp.concatenate(
        [attn_routes, segment_ids.reshape(row_count, 1), jnp.zeros((row_count, 125), jnp.int32)],
        axis=1,
    ).astype(jnp.bfloat16)
    gathered = lax.all_gather(
        jnp.concatenate([normed, labels], axis=1), "head", axis=0, tiled=True
    )
    normed_all = gathered[:, :D]
    labels_all = gathered[:, D : D + 3].astype(jnp.int32)
    routes_all, segment_row = labels_all[:, :2], labels_all[:, 2]
    table = rotary_table(positions(segment_row))
    pair_weights = pair_gates(normed_all, attn_router, routes_all)
    info = jnp.concatenate(
        [
            routes_all.astype(jnp.float32),
            pair_weights,
            segment_row[:, None].astype(jnp.float32),
            jnp.zeros((seq_length, 3), jnp.float32),
        ],
        axis=1,
    ).T
    partial_value = attention(
        normed_all, info, table, w_key, w_value, w_query, w_out, capacity
    )
    attn_rows = lax.psum_scatter(
        partial_value, "head", scatter_dimension=0, tiled=True
    ).astype(jnp.float32)
    residual = (hidden_in.astype(jnp.float32) + attn_rows).astype(jnp.bfloat16)
    ffn_normed = rms_norm(residual, ffn_gain)
    ffn_weights = pair_gates(ffn_normed, ffn_router, ffn_routes)
    cap_ffn = 3 * row_count // 8
    local_experts = w_gate_up.shape[0]
    slot_count = E_FF * cap_ffn
    experts = jnp.arange(E_FF, dtype=jnp.int32)
    member = jnp.sum((ffn_routes[:, :, None] == experts).astype(jnp.float32), axis=1)
    order = jnp.arange(row_count, dtype=jnp.int32)
    earlier = (order[None, :] < order[:, None]).astype(jnp.float32)
    rank = jnp.dot(earlier, member, preferred_element_type=jnp.float32).astype(jnp.int32)
    picks = jnp.sum(
        jnp.where(ffn_routes[:, :, None] == experts, rank[:, None, :], 0), axis=2
    )
    destination = ffn_routes * cap_ffn + picks
    slot_of = destination[:, :, None] == jnp.arange(slot_count, dtype=jnp.int32)
    chosen = jnp.any(slot_of, axis=1).astype(jnp.bfloat16)
    outgoing = jnp.einsum(
        "ts,td->sd", chosen, ffn_normed, preferred_element_type=jnp.float32
    ).astype(jnp.bfloat16).reshape(head_count, local_experts * cap_ffn, D)
    arrived = lax.all_to_all(outgoing, "head", split_axis=0, concat_axis=0, tiled=True)
    shard_rows = lax.all_gather(arrived, "req", axis=0, tiled=True)
    row_total = shard_rows.shape[0]
    grouped = shard_rows.reshape(row_total, local_experts, cap_ffn, D)
    gate_up = jnp.einsum("mecd,edgf->mecgf", grouped, w_gate_up, preferred_element_type=jnp.float32)
    activated = (jax.nn.silu(gate_up[..., 0, :]) * gate_up[..., 1, :]).astype(jnp.bfloat16)
    partials = jnp.einsum(
        "mecf,efd->mecd", activated, w_down, preferred_element_type=jnp.float32
    ).astype(jnp.bfloat16)
    summed = lax.psum_scatter(
        partials.reshape(lax.axis_size("req") * head_count, local_experts * cap_ffn, D),
        "req",
        scatter_dimension=0,
        tiled=True,
    )
    returned = lax.all_to_all(summed, "head", split_axis=0, concat_axis=0, tiled=True)
    mixing = jnp.sum(jnp.where(slot_of, ffn_weights[:, :, None], 0.0), axis=1)
    mixture = jnp.dot(
        mixing,
        returned.reshape(slot_count, D).astype(jnp.float32),
        precision=lax.Precision.HIGHEST,
    )
    return (residual.astype(jnp.float32) + mixture).astype(jnp.bfloat16)


def solution(mesh):
    return jax.shard_map(
        per_device,
        mesh=mesh,
        in_specs=(
            P(("req", "head"), None),
            P("req", "head"),
            P(("req", "head"), None),
            P(("req", "head"), None),
            P(),
            P(),
            P(None, None, "head"),
            P(None, "head"),
            P(None, "head"),
            P(None, "head", None),
            P(),
            P(),
            P("head", None, None, "req"),
            P("head", "req", None),
        ),
        out_specs=P(("req", "head"), None),
        check_vma=False,
    )
```

```python
import functools

import jax
import jax.numpy as jnp
from jax import lax
from jax.experimental import pallas as pl
from jax.experimental.pallas import tpu as pltpu
from jax.sharding import PartitionSpec as P

D = 2048
HD = 128
E_ATT = 8
E_FF = 8


EPSILON = 1e-06
ROPE_BASE = 10000.0


def rms_norm(values, gain_vector):
    widened = values.astype(jnp.float32)
    inverse_rms = lax.rsqrt(jnp.mean(widened * widened, axis=-1, keepdims=True) + EPSILON)
    return (widened * inverse_rms * gain_vector).astype(jnp.bfloat16)


def pair_gates(normed, router, routes):
    logits = jnp.dot(normed.astype(jnp.float32), router, precision=lax.Precision.HIGHEST)
    experts = jnp.arange(router.shape[1], dtype=jnp.int32)
    onehot = (routes[:, :, None] == experts).astype(jnp.float32)
    picked = jnp.sum(onehot * logits[:, None, :], axis=2)
    return jax.nn.sigmoid(picked - picked[:, ::-1])


def positions(segment_row):
    earlier = (segment_row[None, :] < segment_row[:, None]).astype(jnp.int32)
    return jnp.arange(segment_row.shape[0], dtype=jnp.int32) - jnp.sum(earlier, axis=1)


def rotary_table(token_place):
    half_width = HD // 2
    inverse = ROPE_BASE ** (-jnp.arange(half_width, dtype=jnp.float32) / half_width)
    angles = token_place.astype(jnp.float32)[:, None] * inverse
    cosine = jnp.cos(angles)
    sines = jnp.sin(angles)
    return jnp.concatenate([cosine, cosine, -sines, sines], axis=1)


def rotate(head, table):
    return head * table[:, :HD] + pltpu.roll(head, HD // 2, 1) * table[:, HD:]


def attention_kernel(
    capacity, rows_ref, info_ref, table_ref, w_key_ref, w_value_ref, w_query_ref, w_out_ref,
    out_ref, keys, values, total,
):
    expert = pl.program_id(0)
    seq = rows_ref.shape[0]
    heads = w_key_ref.shape[1] // HD
    rows = rows_ref[...]

    @pl.when(expert == 0)
    def _():
        raw_keys = jnp.dot(rows, w_key_ref[...], preferred_element_type=jnp.float32)
        for head in range(heads):
            part = raw_keys[:, head * HD : (head + 1) * HD]
            keys[:, head * HD : (head + 1) * HD] = rotate(part, table_ref[...]).astype(jnp.bfloat16)
        values[...] = jnp.dot(
            rows, w_value_ref[...], preferred_element_type=jnp.float32
        ).astype(jnp.bfloat16)
        total[...] = jnp.zeros_like(total)

    own = expert.astype(jnp.float32)
    first, second = info_ref[0:1, :] == own, info_ref[1:2, :] == own
    member = (first | second).astype(jnp.float32)
    gates = jnp.where(first, info_ref[2:3, :], jnp.where(second, info_ref[3:4, :], 0.0))
    segments = info_ref[4:5, :]
    earlier = (
        lax.broadcasted_iota(jnp.int32, (seq, seq), 0)
        < lax.broadcasted_iota(jnp.int32, (seq, seq), 1)
    ).astype(jnp.float32).astype(jnp.bfloat16)
    rank = jnp.dot(
        jnp.broadcast_to(member, (16, seq)).astype(jnp.bfloat16), earlier,
        preferred_element_type=jnp.float32,
    )[0:1, :]
    slots = lax.broadcasted_iota(jnp.int32, (capacity, seq), 0).astype(jnp.float32)
    place = lax.broadcasted_iota(jnp.int32, (capacity, seq), 1).astype(jnp.float32)
    pick = jnp.where((slots == rank) & (member > 0.0), 1.0, 0.0)
    pick_half = pick.astype(jnp.bfloat16)
    slot_gate = jnp.sum(pick * gates, axis=1, keepdims=True)
    slot_segment = jnp.sum(pick * segments, axis=1, keepdims=True)
    slot_place = jnp.sum(pick * place, axis=1, keepdims=True)
    slot_table = jnp.dot(
        pick, table_ref[...], precision=lax.Precision.HIGHEST, preferred_element_type=jnp.float32
    )
    allowed = (slot_segment == segments) & (place <= slot_place)
    picked = jnp.dot(pick_half, rows, preferred_element_type=jnp.float32).astype(jnp.bfloat16)
    raw = jnp.dot(picked, w_query_ref[0], preferred_element_type=jnp.float32)
    contexts = []
    for head in range(heads):
        span = slice(head * HD, (head + 1) * HD)
        query = rotate(raw[:, span], slot_table).astype(jnp.bfloat16)
        scores = lax.dot_general(
            query, keys[:, span], (((1,), (1,)), ((), ())), preferred_element_type=jnp.float32
        ) * HD ** (-0.5)
        masked = jnp.where(allowed, scores, -1e30)
        exponent = jnp.exp(masked - jnp.max(masked, axis=1, keepdims=True))
        probs = (exponent / jnp.sum(exponent, axis=1, keepdims=True)).astype(jnp.bfloat16)
        contexts.append(
            jnp.dot(probs, values[:, span], preferred_element_type=jnp.float32).astype(jnp.bfloat16)
        )
    context = jnp.concatenate(contexts, axis=1)
    projected = jnp.dot(context, w_out_ref[0], preferred_element_type=jnp.float32)
    weighted = (projected * slot_gate).astype(jnp.bfloat16)
    total[...] += lax.dot_general(
        pick_half, weighted, (((0,), (0,)), ((), ())), preferred_element_type=jnp.float32
    )

    @pl.when(expert == pl.num_programs(0) - 1)
    def _():
        out_ref[...] = total[...].astype(jnp.bfloat16)


def attention(rows, info, table, w_key, w_value, w_query, w_out, capacity):
    seq, width = rows.shape[0], w_key.shape[1]
    whole = lambda shape: pl.BlockSpec(shape, lambda e: (0,) * len(shape))
    return pl.pallas_call(
        functools.partial(attention_kernel, capacity),
        grid=(E_ATT,),
        out_shape=jax.ShapeDtypeStruct((seq, D), jnp.bfloat16),
        in_specs=[
            whole((seq, D)),
            whole(info.shape),
            whole(table.shape),
            whole((D, width)),
            whole((D, width)),
            pl.BlockSpec((1, D, width), lambda e: (e, 0, 0)),
            pl.BlockSpec((1, width, D), lambda e: (e, 0, 0)),
        ],
        out_specs=whole((seq, D)),
        scratch_shapes=[
            pltpu.VMEM((seq, width), jnp.bfloat16),
            pltpu.VMEM((seq, width), jnp.bfloat16),
            pltpu.VMEM((seq, D), jnp.float32),
        ],
        compiler_params=pltpu.CompilerParams(vmem_limit_bytes=48 * 1024 * 1024),
        cost_estimate=pl.CostEstimate(
            flops=12 * 10**9, bytes_accessed=40 * 10**6, transcendentals=10**6
        ),
    )(rows, info, table, w_key, w_value, w_query, w_out)


def exchange(values, step):
    pairs = [(i, i ^ step) for i in range(lax.axis_size("req"))]
    return lax.ppermute(values, "req", pairs)


def spread(block, order):
    stack = block[None]
    for step in order:
        stack = jnp.concatenate([stack, exchange(stack, step)], axis=0)
    return stack


def collect(stack, order):
    for step in order[::-1]:
        kept = stack.shape[0] // 2
        arrived = exchange(stack[kept:], step)
        stack = (stack[:kept].astype(jnp.float32) + arrived.astype(jnp.float32)).astype(
            jnp.bfloat16
        )
    return stack[0]


def per_device(
    hidden_in,
    segment_ids,
    attn_routes,
    ffn_routes,
    attn_gain,
    attn_router,
    w_query,
    w_key,
    w_value,
    w_out,
    ffn_gain,
    ffn_router,
    w_gate_up,
    w_down,
):
    row_count = hidden_in.shape[0]
    head_count = lax.axis_size("head")
    seq_length = row_count * head_count
    capacity = 3 * seq_length // 8
    normed = rms_norm(hidden_in, attn_gain)
    labels = jnp.concatenate(
        [attn_routes, segment_ids.reshape(row_count, 1), jnp.zeros((row_count, 125), jnp.int32)],
        axis=1,
    ).astype(jnp.bfloat16)
    gathered = lax.all_gather(
        jnp.concatenate([normed, labels], axis=1), "head", axis=0, tiled=True
    )
    normed_all = gathered[:, :D]
    labels_all = gathered[:, D : D + 3].astype(jnp.int32)
    routes_all, segment_row = labels_all[:, :2], labels_all[:, 2]
    table = rotary_table(positions(segment_row))
    pair_weights = pair_gates(normed_all, attn_router, routes_all)
    info = jnp.concatenate(
        [
            routes_all.astype(jnp.float32),
            pair_weights,
            segment_row[:, None].astype(jnp.float32),
            jnp.zeros((seq_length, 3), jnp.float32),
        ],
        axis=1,
    ).T
    partial_value = attention(
        normed_all, info, table, w_key, w_value, w_query, w_out, capacity
    )
    attn_rows = lax.psum_scatter(
        partial_value, "head", scatter_dimension=0, tiled=True
    ).astype(jnp.float32)
    residual = (hidden_in.astype(jnp.float32) + attn_rows).astype(jnp.bfloat16)
    ffn_normed = rms_norm(residual, ffn_gain)
    ffn_weights = pair_gates(ffn_normed, ffn_router, ffn_routes)
    cap_ffn = 3 * row_count // 8
    local_experts = w_gate_up.shape[0]
    slot_count = E_FF * cap_ffn
    experts = jnp.arange(E_FF, dtype=jnp.int32)
    member = jnp.sum((ffn_routes[:, :, None] == experts).astype(jnp.float32), axis=1)
    order = jnp.arange(row_count, dtype=jnp.int32)
    earlier = (order[None, :] < order[:, None]).astype(jnp.float32)
    rank = jnp.dot(earlier, member, preferred_element_type=jnp.float32).astype(jnp.int32)
    picks = jnp.sum(
        jnp.where(ffn_routes[:, :, None] == experts, rank[:, None, :], 0), axis=2
    )
    destination = ffn_routes * cap_ffn + picks
    slot_of = destination[:, :, None] == jnp.arange(slot_count, dtype=jnp.int32)
    chosen = jnp.any(slot_of, axis=1).astype(jnp.bfloat16)
    outgoing = jnp.einsum(
        "ts,td->sd", chosen, ffn_normed, preferred_element_type=jnp.float32
    ).astype(jnp.bfloat16).reshape(head_count, local_experts, cap_ffn, D)
    req_count = lax.axis_size("req")
    steps = [1 << bit for bit in range(1, req_count.bit_length() - 1)]
    orders = [steps + [1], steps[::-1] + [1]]
    half_rows = head_count * cap_ffn // 2
    results = []
    for expert in range(local_experts):
        arrived = lax.all_to_all(
            outgoing[:, expert], "head", split_axis=0, concat_axis=0, tiled=True
        ).reshape(2, half_rows, D)
        stacks = [spread(arrived[half], orders[half]) for half in range(2)]
        rows = jnp.concatenate(stacks, axis=0).reshape(-1, D)
        gate_up = jnp.einsum(
            "md,dgf->mgf", rows, w_gate_up[expert], preferred_element_type=jnp.float32
        )
        activated = (jax.nn.silu(gate_up[:, 0]) * gate_up[:, 1]).astype(jnp.bfloat16)
        partials = (
            jnp.dot(activated, w_down[expert], preferred_element_type=jnp.float32)
            .astype(jnp.bfloat16)
            .reshape(2, req_count, half_rows, D)
        )
        summed = jnp.stack([collect(partials[half], orders[half]) for half in range(2)])
        results.append(
            lax.all_to_all(
                summed.reshape(head_count, cap_ffn, D),
                "head",
                split_axis=0,
                concat_axis=0,
                tiled=True,
            )
        )
    returned = jnp.stack(results, axis=1)
    mixing = jnp.sum(jnp.where(slot_of, ffn_weights[:, :, None], 0.0), axis=1)
    mixture = jnp.dot(
        mixing,
        returned.reshape(slot_count, D).astype(jnp.float32),
        precision=lax.Precision.HIGHEST,
    )
    return (residual.astype(jnp.float32) + mixture).astype(jnp.bfloat16)


def solution(mesh):
    return jax.shard_map(
        per_device,
        mesh=mesh,
        in_specs=(
            P(("req", "head"), None),
            P("req", "head"),
            P(("req", "head"), None),
            P(("req", "head"), None),
            P(),
            P(),
            P(None, None, "head"),
            P(None, "head"),
            P(None, "head"),
            P(None, "head", None),
            P(),
            P(),
            P("head", None, None, "req"),
            P("head", "req", None),
        ),
        out_specs=P(("req", "head"), None),
        check_vma=False,
    )
```

```python
import functools

import jax
import jax.numpy as jnp
from jax import lax
from jax.experimental import pallas as pl
from jax.experimental.pallas import tpu as pltpu
from jax.sharding import PartitionSpec as P

D = 2048
HD = 128
E_ATT = 8
E_FF = 8


EPSILON = 1e-06
ROPE_BASE = 10000.0


def rms_norm(values, gain_vector):
    widened = values.astype(jnp.float32)
    inverse_rms = lax.rsqrt(jnp.mean(widened * widened, axis=-1, keepdims=True) + EPSILON)
    return (widened * inverse_rms * gain_vector).astype(jnp.bfloat16)


def pair_gates(normed, router, routes):
    logits = jnp.dot(normed.astype(jnp.float32), router, precision=lax.Precision.HIGHEST)
    experts = jnp.arange(router.shape[1], dtype=jnp.int32)
    onehot = (routes[:, :, None] == experts).astype(jnp.float32)
    picked = jnp.sum(onehot * logits[:, None, :], axis=2)
    return jax.nn.sigmoid(picked - picked[:, ::-1])


def positions(segment_row):
    earlier = (segment_row[None, :] < segment_row[:, None]).astype(jnp.int32)
    return jnp.arange(segment_row.shape[0], dtype=jnp.int32) - jnp.sum(earlier, axis=1)


def rotary_table(token_place):
    half_width = HD // 2
    inverse = ROPE_BASE ** (-jnp.arange(half_width, dtype=jnp.float32) / half_width)
    angles = token_place.astype(jnp.float32)[:, None] * inverse
    cosine = jnp.cos(angles)
    sines = jnp.sin(angles)
    return jnp.concatenate([cosine, cosine, -sines, sines], axis=1)


def rotate(head, table):
    return head * table[:, :HD] + pltpu.roll(head, HD // 2, 1) * table[:, HD:]


def attention_kernel(
    capacity, rows_ref, info_ref, table_ref, w_key_ref, w_value_ref, w_query_ref, w_out_ref,
    out_ref, keys, values, total,
):
    expert = pl.program_id(0)
    seq = rows_ref.shape[0]
    heads = w_key_ref.shape[1] // HD
    rows = rows_ref[...]

    @pl.when(expert == 0)
    def _():
        raw_keys = jnp.dot(rows, w_key_ref[...], preferred_element_type=jnp.float32)
        for head in range(heads):
            part = raw_keys[:, head * HD : (head + 1) * HD]
            keys[:, head * HD : (head + 1) * HD] = rotate(part, table_ref[...]).astype(jnp.bfloat16)
        values[...] = jnp.dot(
            rows, w_value_ref[...], preferred_element_type=jnp.float32
        ).astype(jnp.bfloat16)
        total[...] = jnp.zeros_like(total)

    own = expert.astype(jnp.float32)
    first, second = info_ref[0:1, :] == own, info_ref[1:2, :] == own
    member = (first | second).astype(jnp.float32)
    gates = jnp.where(first, info_ref[2:3, :], jnp.where(second, info_ref[3:4, :], 0.0))
    segments = info_ref[4:5, :]
    earlier = (
        lax.broadcasted_iota(jnp.int32, (seq, seq), 0)
        < lax.broadcasted_iota(jnp.int32, (seq, seq), 1)
    ).astype(jnp.float32).astype(jnp.bfloat16)
    rank = jnp.dot(
        jnp.broadcast_to(member, (16, seq)).astype(jnp.bfloat16), earlier,
        preferred_element_type=jnp.float32,
    )[0:1, :]
    slots = lax.broadcasted_iota(jnp.int32, (capacity, seq), 0).astype(jnp.float32)
    place = lax.broadcasted_iota(jnp.int32, (capacity, seq), 1).astype(jnp.float32)
    pick = jnp.where((slots == rank) & (member > 0.0), 1.0, 0.0)
    pick_half = pick.astype(jnp.bfloat16)
    slot_gate = jnp.sum(pick * gates, axis=1, keepdims=True)
    slot_segment = jnp.sum(pick * segments, axis=1, keepdims=True)
    slot_place = jnp.sum(pick * place, axis=1, keepdims=True)
    slot_table = jnp.dot(
        pick, table_ref[...], precision=lax.Precision.HIGHEST, preferred_element_type=jnp.float32
    )
    allowed = (slot_segment == segments) & (place <= slot_place)
    picked = jnp.dot(pick_half, rows, preferred_element_type=jnp.float32).astype(jnp.bfloat16)
    raw = jnp.dot(picked, w_query_ref[0], preferred_element_type=jnp.float32)
    contexts = []
    for head in range(heads):
        span = slice(head * HD, (head + 1) * HD)
        query = rotate(raw[:, span], slot_table).astype(jnp.bfloat16)
        scores = lax.dot_general(
            query, keys[:, span], (((1,), (1,)), ((), ())), preferred_element_type=jnp.float32
        ) * HD ** (-0.5)
        masked = jnp.where(allowed, scores, -1e30)
        exponent = jnp.exp(masked - jnp.max(masked, axis=1, keepdims=True))
        probs = (exponent / jnp.sum(exponent, axis=1, keepdims=True)).astype(jnp.bfloat16)
        contexts.append(
            jnp.dot(probs, values[:, span], preferred_element_type=jnp.float32).astype(jnp.bfloat16)
        )
    context = jnp.concatenate(contexts, axis=1)
    projected = jnp.dot(context, w_out_ref[0], preferred_element_type=jnp.float32)
    weighted = (projected * slot_gate).astype(jnp.bfloat16)
    total[...] += lax.dot_general(
        pick_half, weighted, (((0,), (0,)), ((), ())), preferred_element_type=jnp.float32
    )

    @pl.when(expert == pl.num_programs(0) - 1)
    def _():
        out_ref[...] = total[...].astype(jnp.bfloat16)


def attention(rows, info, table, w_key, w_value, w_query, w_out, capacity):
    seq, width = rows.shape[0], w_key.shape[1]
    whole = lambda shape: pl.BlockSpec(shape, lambda e: (0,) * len(shape))
    return pl.pallas_call(
        functools.partial(attention_kernel, capacity),
        grid=(E_ATT,),
        out_shape=jax.ShapeDtypeStruct((seq, D), jnp.bfloat16),
        in_specs=[
            whole((seq, D)),
            whole(info.shape),
            whole(table.shape),
            whole((D, width)),
            whole((D, width)),
            pl.BlockSpec((1, D, width), lambda e: (e, 0, 0)),
            pl.BlockSpec((1, width, D), lambda e: (e, 0, 0)),
        ],
        out_specs=whole((seq, D)),
        scratch_shapes=[
            pltpu.VMEM((seq, width), jnp.bfloat16),
            pltpu.VMEM((seq, width), jnp.bfloat16),
            pltpu.VMEM((seq, D), jnp.float32),
        ],
        compiler_params=pltpu.CompilerParams(vmem_limit_bytes=48 * 1024 * 1024),
        cost_estimate=pl.CostEstimate(
            flops=12 * 10**9, bytes_accessed=40 * 10**6, transcendentals=10**6
        ),
    )(rows, info, table, w_key, w_value, w_query, w_out)


def exchange(values, step, axis):
    pairs = [(i, i ^ step) for i in range(lax.axis_size(axis))]
    return lax.ppermute(values, axis, pairs)


def shuffled(stack, places):
    return jnp.concatenate(
        [lax.dynamic_index_in_dim(stack, place, 0, keepdims=True) for place in places], axis=0
    )


def spread(block, order, axis="req"):
    stack = block[None]
    for step in order:
        stack = jnp.concatenate([stack, exchange(stack, step, axis)], axis=0)
    return stack


def collect(stack, order, axis="req"):
    for step in order[::-1]:
        kept = stack.shape[0] // 2
        arrived = exchange(stack[kept:], step, axis)
        stack = (stack[:kept].astype(jnp.float32) + arrived.astype(jnp.float32)).astype(
            jnp.bfloat16
        )
    return stack[0]


def per_device(
    hidden_in,
    segment_ids,
    attn_routes,
    ffn_routes,
    attn_gain,
    attn_router,
    w_query,
    w_key,
    w_value,
    w_out,
    ffn_gain,
    ffn_router,
    w_gate_up,
    w_down,
):
    row_count = hidden_in.shape[0]
    head_count = lax.axis_size("head")
    seq_length = row_count * head_count
    capacity = 3 * seq_length // 8
    normed = rms_norm(hidden_in, attn_gain)
    labels = jnp.concatenate(
        [attn_routes, segment_ids.reshape(row_count, 1), jnp.zeros((row_count, 125), jnp.int32)],
        axis=1,
    ).astype(jnp.bfloat16)
    head_order = [1 << bit for bit in range(head_count.bit_length() - 1)][::-1]
    masks = [0]
    for step in head_order:
        masks = masks + [mask | step for mask in masks]
    head_index = lax.axis_index("head")
    held_at = jnp.array([masks.index(mask) for mask in range(head_count)], jnp.int32)
    stack = spread(jnp.concatenate([normed, labels], axis=1), head_order, "head")
    gathered = shuffled(
        stack, [held_at[head_index ^ place] for place in range(head_count)]
    ).reshape(seq_length, -1)
    normed_all = gathered[:, :D]
    labels_all = gathered[:, D : D + 3].astype(jnp.int32)
    routes_all, segment_row = labels_all[:, :2], labels_all[:, 2]
    table = rotary_table(positions(segment_row))
    pair_weights = pair_gates(normed_all, attn_router, routes_all)
    info = jnp.concatenate(
        [
            routes_all.astype(jnp.float32),
            pair_weights,
            segment_row[:, None].astype(jnp.float32),
            jnp.zeros((seq_length, 3), jnp.float32),
        ],
        axis=1,
    ).T
    partial_value = attention(
        normed_all, info, table, w_key, w_value, w_query, w_out, capacity
    )
    blocks = partial_value.reshape(head_count, row_count, D)
    attn_rows = collect(
        shuffled(blocks, [head_index ^ mask for mask in masks]), head_order, "head"
    ).astype(jnp.float32)
    residual = (hidden_in.astype(jnp.float32) + attn_rows).astype(jnp.bfloat16)
    ffn_normed = rms_norm(residual, ffn_gain)
    ffn_weights = pair_gates(ffn_normed, ffn_router, ffn_routes)
    cap_ffn = 3 * row_count // 8
    local_experts = w_gate_up.shape[0]
    slot_count = E_FF * cap_ffn
    experts = jnp.arange(E_FF, dtype=jnp.int32)
    member = jnp.sum((ffn_routes[:, :, None] == experts).astype(jnp.float32), axis=1)
    order = jnp.arange(row_count, dtype=jnp.int32)
    earlier = (order[None, :] < order[:, None]).astype(jnp.float32)
    rank = jnp.dot(earlier, member, preferred_element_type=jnp.float32).astype(jnp.int32)
    picks = jnp.sum(
        jnp.where(ffn_routes[:, :, None] == experts, rank[:, None, :], 0), axis=2
    )
    destination = ffn_routes * cap_ffn + picks
    slot_of = destination[:, :, None] == jnp.arange(slot_count, dtype=jnp.int32)
    chosen = jnp.any(slot_of, axis=1).astype(jnp.bfloat16)
    outgoing = jnp.einsum(
        "ts,td->sd", chosen, ffn_normed, preferred_element_type=jnp.float32
    ).astype(jnp.bfloat16).reshape(head_count, local_experts, cap_ffn, D)
    req_count = lax.axis_size("req")
    steps = [1 << bit for bit in range(1, req_count.bit_length() - 1)]
    orders = [steps + [1], steps[::-1] + [1]]
    half_rows = head_count * cap_ffn // 2
    results = []
    for expert in range(local_experts):
        arrived = lax.all_to_all(
            outgoing[:, expert], "head", split_axis=0, concat_axis=0, tiled=True
        ).reshape(2, half_rows, D)
        stacks = [spread(arrived[half], orders[half]) for half in range(2)]
        rows = jnp.concatenate(stacks, axis=0).reshape(-1, D)
        gate_up = jnp.einsum(
            "md,dgf->mgf", rows, w_gate_up[expert], preferred_element_type=jnp.float32
        )
        activated = (jax.nn.silu(gate_up[:, 0]) * gate_up[:, 1]).astype(jnp.bfloat16)
        partials = (
            jnp.dot(activated, w_down[expert], preferred_element_type=jnp.float32)
            .astype(jnp.bfloat16)
            .reshape(2, req_count, half_rows, D)
        )
        summed = jnp.stack([collect(partials[half], orders[half]) for half in range(2)])
        results.append(
            lax.all_to_all(
                summed.reshape(head_count, cap_ffn, D),
                "head",
                split_axis=0,
                concat_axis=0,
                tiled=True,
            )
        )
    returned = jnp.stack(results, axis=1)
    mixing = jnp.sum(jnp.where(slot_of, ffn_weights[:, :, None], 0.0), axis=1)
    mixture = jnp.dot(
        mixing,
        returned.reshape(slot_count, D).astype(jnp.float32),
        precision=lax.Precision.HIGHEST,
    )
    return (residual.astype(jnp.float32) + mixture).astype(jnp.bfloat16)


def solution(mesh):
    return jax.shard_map(
        per_device,
        mesh=mesh,
        in_specs=(
            P(("req", "head"), None),
            P("req", "head"),
            P(("req", "head"), None),
            P(("req", "head"), None),
            P(),
            P(),
            P(None, None, "head"),
            P(None, "head"),
            P(None, "head"),
            P(None, "head", None),
            P(),
            P(),
            P("head", None, None, "req"),
            P("head", "req", None),
        ),
        out_specs=P(("req", "head"), None),
        check_vma=False,
    )
```
